32 devices in a mesh: pool: 4 (over y, x), section: 2 (over core), tensor: 4 (over z).
Axes of the slice: x: 2, y: 2, z: 4, core: 2. Of those that a mesh axis runs over, the one named last changes fastest.
Arguments:
- hidden_input: bfloat16 [2048, 8192], P('pool', 'tensor'), may hold values from -6 to 6
- attention_output: bfloat16 [2, 2048, 8192], P('section', 'pool', 'tensor'), may hold values from -6 to 6
- projection_weight: bfloat16 [2, 8192, 8192], P('section', 'tensor'), may hold values from -0.09375 to 0.09375
- lowrank_down_factor: bfloat16 [2, 128, 64, 8192], P('section', 'pool', None, 'tensor'), may hold values from -0.0625 to 0.0625
- lowrank_up_factor: bfloat16 [2, 128, 64, 8192], P('section', 'pool', None, 'tensor'), may hold values from -0.75 to 0.75
- residual_block_mats: bfloat16 [2, 128, 4, 128, 128], P('section', 'pool', 'tensor'), may hold values from -0.5 to 0.5
- diagonal_block_index: int32 [2, 128, 4], P('section', 'pool', 'tensor'), may hold values from 0 to 63, as said below
- row_variant_index: int32 [2048], P('pool'), may hold values from 0 to 127, as said below
Outputs:
- hidden_out: bfloat16 [2, 2048, 8192], P('section', 'pool', 'tensor')
The draws below stay inside these ranges and needn't reach their ends.
Inputs may be any that keep to these rules, and one draw needn't show every extreme that they name: `row_variant_index`: within each aligned block of 512 rows the ids never fall; at most 256 rows of a block name variants of one owner q (ids q * 32 to (q + 1) * 32 - 1), and some owner receives exactly 256 rows from every block. `diagonal_block_index`: entry j of each list lies in j * 16 to (j + 1) * 16 - 1.
All inputs are finite; a program needn't handle non-finite values.
Results may differ from the reference program's by a relative error of at most 0.017.
Values may be sent and summed in bfloat16 or wider, within the bound.
A program may use at most 128 MiB of HBM per device.

```python
import math
import jax
import jax.numpy as jnp
from jax import lax

MODEL_WIDTH = 8192
DELTA_RANK = 64
BLK = 128
VAR_DEV = 32
ROWS_DEV = 512
LAYER_COUNT = 2
FEAT_GROUPS = 4
NBLK = 4
BPS = 16
POOLS = 4
VARIANT_COUNT = 128
ROWS = 2048
CAP = 256


def draw_row_variant_index(key, part):
    base_key = jax.random.fold_in(key, 17)
    hot_key, owner_key, local_key = jax.random.split(base_key, 3)
    hot_owner = jax.random.randint(hot_key, (), 0, POOLS)
    others = jax.random.randint(owner_key, (POOLS, ROWS_DEV), 0, POOLS - 1)
    others = others + (others >= hot_owner).astype(jnp.int32)
    position = jnp.arange(ROWS_DEV)[None, :]
    owners = jnp.where(position < CAP, hot_owner, others)
    local_var = jax.random.randint(local_key, (POOLS, ROWS_DEV), 0, VAR_DEV)
    chosen = jnp.sort(owners * VAR_DEV + local_var, axis=1)
    return chosen.reshape(ROWS).astype(jnp.int32)


def draw_diagonal_block_index(key, part):
    offsets = jax.random.randint(jax.random.fold_in(key, 29), (LAYER_COUNT, VARIANT_COUNT, NBLK), 0, BPS)
    return (jnp.arange(NBLK, dtype=jnp.int32)[None, None, :] * BPS + offsets).astype(jnp.int32)


def strengthened(entries, own_key, source, target, parts, factor):
    owner, partner = [(jnp.arange(entries.shape[dim]) // (entries.shape[dim] // parts)).reshape([-1 if axis == dim else 1 for axis in range(entries.ndim)]) for dim in (source, target)]
    chosen = jax.random.permutation(own_key, parts)[partner]
    strong = (owner == chosen) | (owner == (partner + parts // 2) % parts)
    return jnp.where(strong, factor * entries, entries)


def level_of(rng, shape, cuts, least, top_value):
    gain, own = 1.0, jax.random.fold_in(rng, 6)
    for axis_at, blocks in cuts:
        steps = jnp.exp(jax.random.uniform(jax.random.fold_in(own, axis_at), (blocks,), jnp.float32, least / len(cuts), top_value / len(cuts)))
        gain = gain * jnp.repeat(steps, shape[axis_at] // blocks).reshape([-1 if axis == axis_at else 1 for axis in range(len(shape))])
    return gain


def centred(key, dims, deviation, limit, cuts=(), held_as=jnp.bfloat16):
    factor_of = level_of(key, dims, cuts, -0.22, 0.18) if cuts else 1.0
    array = jax.random.normal(key, dims, jnp.float32) * deviation * factor_of
    return jnp.minimum(jnp.maximum(array, -limit), limit).astype(held_as)


def bell_draw_with(rng, shape, deviation, most, pieces, heavy, held_as=jnp.bfloat16):
    result = deviation * jax.random.normal(rng, shape, jnp.float32)
    if pieces:
        result = result * level_of(rng, shape, pieces, -0.22, 0.18)
    return jnp.clip(strengthened(result, jax.random.fold_in(rng, 3), *heavy), -most, most).astype(held_as)


def setup_inputs(seed: int = 0) -> dict:
    splits = jax.random.split(jax.random.key(seed), 9)
    return {
        "hidden_input": centred(splits[0], (ROWS, MODEL_WIDTH), 1.0, 6.0, ((0, 4), (1, 4))),
        "attention_output": centred(splits[1], (LAYER_COUNT, ROWS, MODEL_WIDTH), 1.0, 6.0, ((0, 2), (1, 4), (2, 4))),
        "projection_weight": bell_draw_with(splits[2], (LAYER_COUNT, MODEL_WIDTH, MODEL_WIDTH), MODEL_WIDTH ** -0.5, 0.09375, ((0, 2), (1, 4)), (1, 2, 4, 2.0)),
        "lowrank_down_factor": centred(splits[3], (LAYER_COUNT, VARIANT_COUNT, DELTA_RANK, MODEL_WIDTH), MODEL_WIDTH ** -0.5, 0.0625, ((0, 2), (1, 4), (3, 4))),
        "lowrank_up_factor": centred(splits[4], (LAYER_COUNT, VARIANT_COUNT, DELTA_RANK, MODEL_WIDTH), DELTA_RANK ** -0.5, 0.75, ((0, 2), (1, 4), (3, 4))),
        "residual_block_mats": centred(splits[5], (LAYER_COUNT, VARIANT_COUNT, NBLK, BLK, BLK), BLK ** -0.5, 0.5, ((0, 2), (1, 4), (2, 4))),
        "diagonal_block_index": draw_diagonal_block_index(jax.random.fold_in(splits[8], 71), 0),
        "row_variant_index": draw_row_variant_index(jax.random.fold_in(splits[8], 71), 0),
    }


def group_sum(features, weight):
    group_width = MODEL_WIDTH // FEAT_GROUPS
    feat_groups = jnp.transpose(features.reshape(ROWS, FEAT_GROUPS, group_width), (1, 0, 2))
    weight_groups = weight.reshape(FEAT_GROUPS, group_width, MODEL_WIDTH)

    def add_group(running, operands):
        feat_part, weight_part = operands
        product = jnp.dot(feat_part, weight_part, preferred_element_type=jnp.float32).astype(jnp.bfloat16)
        product = lax.optimization_barrier(product)
        return running + product.astype(jnp.float32), None

    return lax.scan(add_group, jnp.zeros((ROWS, MODEL_WIDTH), jnp.float32), (feat_groups, weight_groups))[0]


def adapter_row_values(features, row_vars, down_all, up_all, block_all, index_all):
    row_block = math.gcd(ROWS, 64)
    feat_split = features.reshape(ROWS // row_block, row_block, MODEL_WIDTH)
    var_split = row_vars.reshape(ROWS // row_block, row_block)

    def one_block(operands):
        feat_rows, block_vars = operands
        down_factor_rows = jnp.take(down_all, block_vars, axis=0)
        lowrank_product = jnp.einsum("rkd,rd->rk", down_factor_rows.astype(jnp.float32), feat_rows.astype(jnp.float32)).astype(jnp.bfloat16)
        up_factor_rows = jnp.take(up_all, block_vars, axis=0)
        lowrank_output = jnp.einsum("la,lat->lt", lowrank_product.astype(jnp.float32), up_factor_rows.astype(jnp.float32))
        block_mats = jnp.take(block_all, block_vars, axis=0)
        places = jnp.take(index_all, block_vars, axis=0).astype(jnp.int32)
        feat_blocks = feat_rows.reshape(row_block, MODEL_WIDTH // BLK, BLK)
        picked = jnp.take_along_axis(feat_blocks, places[:, :, None], axis=1)
        block_y = jnp.einsum("rjk,rjkm->rjm", picked.astype(jnp.float32), block_mats.astype(jnp.float32))
        place_hot = (places[:, :, None] == jnp.arange(MODEL_WIDTH // BLK, dtype=jnp.int32)[None, None, :]).astype(jnp.float32)
        block_output = jnp.einsum("rjm,rjb->rbm", block_y, place_hot).reshape(row_block, MODEL_WIDTH)
        return (lowrank_output + block_output).astype(jnp.bfloat16)

    return lax.map(one_block, (feat_split, var_split)).reshape(ROWS, MODEL_WIDTH)


def reference(hidden_input, attention_output, projection_weight, lowrank_down_factor, lowrank_up_factor, residual_block_mats, diagonal_block_index, row_variant_index):
    current = hidden_input
    outputs = []
    for layer_number in range(LAYER_COUNT):
        base_sum = group_sum(attention_output[layer_number], projection_weight[layer_number])
        adapter_output = adapter_row_values(attention_output[layer_number], row_variant_index, lowrank_down_factor[layer_number], lowrank_up_factor[layer_number], residual_block_mats[layer_number], diagonal_block_index[layer_number])
        current = (current.astype(jnp.float32) + base_sum + adapter_output.astype(jnp.float32)).astype(jnp.bfloat16)
        outputs.append(current)
    return jnp.stack(outputs)
```

```python
import functools
import math

import jax
import jax.numpy as jnp
from jax import lax
from jax.experimental import pallas as pl
from jax.experimental.pallas import tpu as pltpu
from jax.sharding import PartitionSpec as P

LANES = 128
LAG = 2
WINDOW = 3
BF16 = jnp.bfloat16
F32 = jnp.float32


def remote(src, dst, send_sem, recv_sem, **where):
    return pltpu.make_async_remote_copy(
        src_ref=src,
        dst_ref=dst,
        send_sem=send_sem,
        recv_sem=recv_sem,
        device_id=where,
        device_id_type=pl.DeviceIdType.MESH,
    )


def fused(
    cfg,
    feat, hidden, weight, down, up, mats, source, slot, var_send, place_tab,
    out,
    rbuf, wbuf, tmp, acc, sendf, recvf, retf, lowbuf, varbuf, comb, secbuf,
    lracc, lrp, pre_in, suf_in, pre_out, suf_out, yterm, placef, pickb,
    w_sem, low_sem, rs_send, rs_recv, a2a_send, a2a_recv, var_ssem, var_rsem,
    ret_send, ret_recv, lr_send, lr_recv, sec_send, sec_recv,
):
    n, pools, sections, rank, cw, tile = cfg
    rows, width = feat.shape
    groups = width // cw
    slots = recvf.shape[0]
    cap = slots // pools
    reps = LANES // rank
    low_rows = lowbuf.shape[0]
    i = lax.axis_index("tensor")
    me = lax.axis_index("pool")
    sec = lax.axis_index("section")
    seqs = (n - 1) * groups
    plus_at = (n - 1 - i) * groups + LAG * i
    minus_at = i * groups + LAG * (n - 1 - i)
    plus_first = (i > 0) & ((i == n - 1) | (plus_at <= minus_at))

    def low_copy(src):
        return pltpu.make_async_copy(src, lowbuf, low_sem)

    def parts(step, direction):
        lag_pos = i if direction == 0 else n - 1 - i
        seq = step - LAG * lag_pos
        valid = (seq >= 0) & (seq < seqs)
        seq = jnp.clip(seq, 0, seqs - 1)
        phase, chunk = seq // groups, seq % groups
        if direction == 0:
            target = n - 1 - phase
            sends = valid & (target > i)
            keeps = valid & (target == i)
            first = keeps & plus_first
            receives = i > 0
            index = target * groups + chunk
        else:
            target = phase
            sends = valid & (target < i)
            keeps = valid & (target == i)
            first = keeps & jnp.logical_not(plus_first)
            receives = i < n - 1
            index = jnp.where(target == i, n, target) * groups + chunk
        return seq, target, chunk, sends, keeps, first, receives, index

    def weight_copy(step, direction):
        _, target, chunk, _, _, _, _, _ = parts(step, direction)
        column = pl.multiple_of(target * width + chunk * cw, cw)
        return pltpu.make_async_copy(
            weight.at[:, pl.ds(column, cw)],
            wbuf.at[step % 2, direction],
            w_sem.at[step % 2, direction],
        )

    def fetch(step):
        for direction in range(2):
            _, _, _, sends, _, first, _, _ = parts(step, direction)

            @pl.when(sends | first)
            def _():
                weight_copy(step, direction).start()

    def rs_copy(direction, index):
        to = i + 1 if direction == 0 else i - 1
        return remote(
            rbuf.at[index], rbuf.at[index], rs_send.at[index], rs_recv.at[index],
            tensor=jnp.clip(to, 0, n - 1),
        )

    def rs_out(direction, seq):
        phase, chunk = seq // groups, seq % groups
        target = n - 1 - phase if direction == 0 else phase
        index = target * groups + chunk
        to = i + 1 if direction == 0 else i - 1
        landing = index
        if direction == 1:
            landing = jnp.where(target == to, n, target) * groups + chunk
        return remote(
            rbuf.at[index], rbuf.at[landing], rs_send.at[index], rs_recv.at[landing],
            tensor=jnp.clip(to, 0, n - 1),
        )

    def step_body(step):
        @pl.when(step + 1 < total_steps)
        def _():
            fetch(step + 1)

        for direction in range(2):
            seq, _, chunk, sends, keeps, first, receives, index = parts(step, direction)

            @pl.when(sends | first)
            def _():
                weight_copy(step, direction).wait()
                tmp[...] = jnp.dot(
                    feat[...], wbuf[step % 2, direction], preferred_element_type=F32
                )

            @pl.when((sends | keeps) & receives)
            def _():
                rs_copy(direction, index).wait_recv()

            @pl.when(sends)
            def _():
                @pl.when(receives)
                def _():
                    rbuf[index] = (tmp[...] + rbuf[index].astype(F32)).astype(BF16)

                @pl.when(jnp.logical_not(receives))
                def _():
                    rbuf[index] = tmp[...].astype(BF16)

                @pl.when(seq >= WINDOW)
                def _():
                    rs_out(direction, seq - WINDOW).wait_send()

                rs_out(direction, seq).start()

            @pl.when(first & receives)
            def _():
                acc[chunk] = tmp[...] + rbuf[index].astype(F32)

            @pl.when(first & jnp.logical_not(receives))
            def _():
                acc[chunk] = tmp[...]

            @pl.when(keeps & receives & jnp.logical_not(first))
            def _():
                acc[chunk] = acc[chunk] + rbuf[index].astype(F32)

    per_step = 2
    adapt_at = max(1, 3 * seqs // 8)
    hops_end = adapt_at + n - 1
    served_at = hops_end + pl.cdiv(groups, per_step)
    finals = [
        max((n - 1 - p) * groups + LAG * p, p * groups + LAG * (n - 1 - p), served_at)
        for p in range(n)
    ]
    total_steps = max(finals) + groups
    final_at = jnp.maximum(jnp.maximum(plus_at, minus_at), served_at)

    def sec_copy(chunk):
        cols = pl.ds(pl.multiple_of(chunk * cw, cw), cw)
        return remote(
            out.at[:, cols], secbuf.at[:, cols], sec_send.at[chunk], sec_recv.at[chunk],
            section=jnp.minimum(sec + 1, sections - 1),
        )

    def ret_copy(chunk, d):
        to = (me + d) % pools
        cols = pl.ds(pl.multiple_of(chunk * cw, cw), cw)
        return remote(
            recvf.at[pl.ds(pl.multiple_of(to * cap, cap), cap), cols],
            retf.at[pl.ds(pl.multiple_of(me * cap, cap), cap), cols],
            ret_send.at[chunk, to],
            ret_recv.at[chunk, me],
            pool=to,
        )

    def ret_arrival(chunk, d):
        owner = (me + d) % pools
        cols = pl.ds(pl.multiple_of(chunk * cw, cw), cw)
        return remote(
            recvf.at[pl.ds(pl.multiple_of(owner * cap, cap), cap), cols],
            retf.at[pl.ds(pl.multiple_of(owner * cap, cap), cap), cols],
            ret_send.at[chunk, owner],
            ret_recv.at[chunk, owner],
            pool=owner,
        )

    def finish(chunk):
        cols = pl.ds(pl.multiple_of(chunk * cw, cw), cw)
        for d in range(1, pools):
            ret_arrival(chunk, d).wait_recv()
        tmp[...] = acc[chunk] + jnp.dot(comb[...], retf[:, cols], preferred_element_type=F32)

        @pl.when(sec == 0)
        def _():
            out[:, cols] = (hidden[:, cols].astype(F32) + tmp[...]).astype(BF16)

        @pl.when(sec > 0)
        def _():
            sec_copy(chunk).wait_recv()
            out[:, cols] = (secbuf[:, cols].astype(F32) + tmp[...]).astype(BF16)

        @pl.when(sec < sections - 1)
        def _():
            sec_copy(chunk).start()

    def steps(first, last):
        @pl.loop(first, last)
        def _(step):
            step_body(step)
            chunk = step - final_at

            @pl.when((chunk >= 0) & (chunk < groups))
            def _():
                finish(chunk)

    def row_copy(d):
        to = (me + d) % pools
        return remote(
            sendf.at[pl.ds(pl.multiple_of(to * cap, cap), cap), pl.ds(0, width)],
            recvf.at[pl.ds(pl.multiple_of(me * cap, cap), cap)],
            a2a_send.at[to], a2a_recv.at[me], pool=to,
        )

    def var_copy(d):
        to = (me + d) % pools
        return remote(
            var_send.at[pl.ds(pl.multiple_of(to * cap, cap), cap)],
            varbuf.at[pl.ds(pl.multiple_of(me * cap, cap), cap)],
            var_ssem.at[to], var_rsem.at[me], pool=to,
        )

    def arrival(d):
        owner = (me + d) % pools
        block = pl.ds(pl.multiple_of(owner * cap, cap), cap)
        return (
            remote(sendf.at[block, pl.ds(0, width)], recvf.at[block], a2a_send.at[owner], a2a_recv.at[owner], pool=owner),
            remote(var_send.at[block], varbuf.at[block], var_ssem.at[owner], var_rsem.at[owner], pool=owner),
        )

    def pre_copy():
        return remote(pre_out, pre_in, lr_send.at[0], lr_recv.at[0],
                      tensor=jnp.minimum(i + 1, n - 1))

    def suf_copy():
        return remote(suf_out, suf_in, lr_send.at[1], lr_recv.at[1],
                      tensor=jnp.maximum(i - 1, 0))

    barrier = pltpu.get_barrier_semaphore()
    for d in range(1, pools):
        pl.semaphore_signal(barrier, inc=1, device_id={"pool": (me + d) % pools},
                            device_id_type=pl.DeviceIdType.MESH)
    for d in range(1, sections):
        pl.semaphore_signal(barrier, inc=1, device_id={"section": (sec + d) % sections},
                            device_id_type=pl.DeviceIdType.MESH)

    @pl.when(i > 0)
    def _():
        pl.semaphore_signal(barrier, inc=1, device_id={"tensor": jnp.maximum(i - 1, 0)},
                            device_id_type=pl.DeviceIdType.MESH)

    @pl.when(i < n - 1)
    def _():
        pl.semaphore_signal(barrier, inc=1, device_id={"tensor": jnp.minimum(i + 1, n - 1)},
                            device_id_type=pl.DeviceIdType.MESH)

    fetch(0)
    low_copy(down).start()
    pl.semaphore_wait(
        barrier,
        pools - 1 + sections - 1 + (i > 0).astype(jnp.int32) + (i < n - 1).astype(jnp.int32),
    )

    steps(0, 1)

    def dispatch(owner, into):
        block = pl.ds(pl.multiple_of(owner * cap, cap), cap)
        pick = (
            source[block, :] == lax.broadcasted_iota(jnp.int32, (cap, rows), 1)
        ).astype(F32).astype(BF16)

        @pl.loop(0, groups)
        def _(chunk):
            cols = pl.ds(pl.multiple_of(chunk * cw, cw), cw)
            into[block, cols] = jnp.dot(
                pick, feat[:, cols], preferred_element_type=F32
            ).astype(BF16)

    for d in range(1, pools):
        var_copy(d).start()

    @pl.loop(1, pools)
    def _(d):
        dispatch((me + d) % pools, sendf)
        row_copy(d).start()

    dispatch(me, recvf)
    own = pl.ds(pl.multiple_of(me * cap, cap), cap)
    varbuf[own, :] = var_send[own, :]
    comb[...] = (
        slot[...] == lax.broadcasted_iota(jnp.int32, (rows, slots), 1)
    ).astype(F32).astype(BF16)

    steps(1, adapt_at)

    for d in range(1, pools):
        rows_in, vars_in = arrival(d)
        rows_in.wait_recv()
        vars_in.wait_recv()
    low_copy(down).wait()
    lane = lax.broadcasted_iota(jnp.int32, (slots, LANES), 1)
    lane_var = (lane // rank).astype(F32)
    per_tile = tile // LANES
    lracc[...] = jnp.zeros_like(lracc)

    @pl.loop(0, low_rows // tile)
    def _(t):
        product = lax.dot_general(
            recvf[...], lowbuf[pl.ds(pl.multiple_of(t * tile, tile), tile), :],
            (((1,), (1,)), ((), ())), preferred_element_type=F32,
        )
        base_var = varbuf[...].astype(F32) - lane_var
        total = lracc[...]
        for b in range(per_tile):
            wanted = ((t * per_tile + b) * reps).astype(F32)
            total = total + jnp.where(
                base_var == wanted, product[:, b * LANES:(b + 1) * LANES], 0.0
            )
        lracc[...] = total

    low_copy(up).start()
    folded = lracc[...]
    for j in range(1, reps):
        folded = folded + pltpu.roll(lracc[...], j * rank, 1)
    packed_rows = slots // reps
    lane_p = lax.broadcasted_iota(jnp.int32, (packed_rows, LANES), 1) // rank
    packed = jnp.zeros((packed_rows, LANES), F32)
    for j in range(reps):
        packed = jnp.where(lane_p == j, folded[j * packed_rows:(j + 1) * packed_rows], packed)
    lrp[...] = packed

    def hop(h):
        @pl.when(i == h)
        def _():
            @pl.when(i > 0)
            def _():
                pre_copy().wait_recv()

            @pl.when(i == 0)
            def _():
                pre_out[...] = lrp[...].astype(BF16)

            @pl.when((i > 0) & (i < n - 1))
            def _():
                pre_out[...] = (lrp[...] + pre_in[...].astype(F32)).astype(BF16)

            @pl.when(i < n - 1)
            def _():
                pre_copy().start()

        @pl.when(n - 1 - i == h)
        def _():
            @pl.when(i < n - 1)
            def _():
                suf_copy().wait_recv()

            @pl.when(i == n - 1)
            def _():
                suf_out[...] = lrp[...].astype(BF16)

            @pl.when((i > 0) & (i < n - 1))
            def _():
                suf_out[...] = (lrp[...] + suf_in[...].astype(F32)).astype(BF16)

            @pl.when(i > 0)
            def _():
                suf_copy().start()

    hop(0)

    hot = (varbuf[...].astype(F32) == lane.astype(F32)).astype(F32).astype(BF16)
    placef[...] = jnp.dot(hot, place_tab[...], preferred_element_type=F32)
    yterm[...] = jnp.zeros_like(yterm)

    @pl.loop(0, width // LANES)
    def _(p):
        block = recvf[:, pl.ds(pl.multiple_of(p * LANES, LANES), LANES)].astype(F32)
        yterm[...] = jnp.where(placef[...] == p.astype(F32), block, yterm[...])

    pickb[...] = yterm[...]
    yterm[...] = jnp.zeros_like(yterm)
    bunch = math.gcd(4, mats.shape[0] // LANES)
    bunch_rows = bunch * LANES

    @pl.loop(0, mats.shape[0] // bunch_rows)
    def _(g):
        masked = [
            jnp.where(
                varbuf[...].astype(F32) == (g * bunch + b).astype(F32), pickb[...], 0.0
            ).astype(BF16)
            for b in range(bunch)
        ]
        yterm[...] += jnp.dot(
            jnp.concatenate(masked, axis=1),
            mats[pl.ds(pl.multiple_of(g * bunch_rows, bunch_rows), bunch_rows), :],
            preferred_element_type=F32,
        )

    @pl.loop(1, n)
    def _(h):
        steps(adapt_at + h - 1, adapt_at + h)
        hop(h)

    @pl.when(i > 0)
    def _():
        lrp[...] += pre_in[...].astype(F32)

    @pl.when(i < n - 1)
    def _():
        lrp[...] += suf_in[...].astype(F32)

    for d in range(1, pools):
        row_copy(d).wait_send()
        var_copy(d).wait_send()
    for j in range(reps):
        mine = jnp.where(lane_p == j, lrp[...], 0.0)
        spread = mine
        for k in range(1, reps):
            spread = spread + pltpu.roll(mine, k * rank, 1)
        spread = spread.astype(BF16)
        block = pl.ds(j * packed_rows, packed_rows)
        base_var = varbuf[block, :].astype(F32) - lane_p.astype(F32)
        for b in range(low_rows // LANES):
            sendf[block, b * LANES:(b + 1) * LANES] = jnp.where(
                base_var == float(b * reps), spread, 0.0
            ).astype(BF16)
    low_copy(up).wait()

    def serve(chunk):
        cols = pl.ds(pl.multiple_of(chunk * cw, cw), cw)
        answer = jnp.dot(sendf[:, 0:low_rows], lowbuf[:, cols], preferred_element_type=F32)
        placed = [
            jnp.where(placef[...] == (chunk * (cw // LANES) + b).astype(F32), yterm[...], 0.0)
            for b in range(cw // LANES)
        ]
        recvf[:, cols] = (answer + jnp.concatenate(placed, axis=1)).astype(BF16)
        for d in range(1, pools):
            ret_copy(chunk, d).start()
        retf[own, cols] = recvf[own, cols]

    per_step = 2
    @pl.loop(0, groups)
    def _(chunk):
        serve(chunk)

        @pl.when(chunk % per_step == per_step - 1)
        def _():
            at = hops_end + chunk // per_step
            steps(at, at + 1)

    steps(hops_end + groups // per_step, total_steps)

    for direction in range(2):
        count = ((n - 1 - i) if direction == 0 else i) * groups

        @pl.loop(jnp.maximum(count - WINDOW, 0), count)
        def _(seq):
            rs_out(direction, seq).wait_send()

    @pl.when(i < n - 1)
    def _():
        pre_copy().wait_send()

    @pl.when(i > 0)
    def _():
        suf_copy().wait_send()

    @pl.loop(0, groups)
    def _(chunk):
        for d in range(1, pools):
            ret_copy(chunk, d).wait_send()

        @pl.when(sec < sections - 1)
        def _():
            sec_copy(chunk).wait_send()


def per_device(
    mesh,
    hidden_input,
    attention_output,
    projection_weight,
    lowrank_down_factor,
    lowrank_up_factor,
    residual_block_mats,
    diagonal_block_index,
    row_variant_index,
):
    n, pools, sections = mesh.shape["tensor"], mesh.shape["pool"], mesh.shape["section"]
    feat, weight = attention_output[0], projection_weight[0]
    down, up, mats = lowrank_down_factor[0], lowrank_up_factor[0], residual_block_mats[0][:, 0]
    rows, width = feat.shape
    variants, rank, _ = down.shape
    block = mats.shape[-1]
    low_rows = variants * rank
    cap = rows // 2
    slots = pools * cap
    cw = min(256, width)
    groups = width // cw
    tile = min(256, low_rows)
    reps = LANES // rank
    per_shard = width // block

    owners = row_variant_index // variants
    owner_hot = (owners[:, None] == jnp.arange(pools)[None, :]).astype(jnp.int32)
    counts = jnp.sum(owner_hot, axis=0)
    starts = jnp.cumsum(counts) - counts
    position = jnp.arange(rows) - jnp.sum(owner_hot * starts[None, :], axis=1)
    slot = (owners * cap + position).astype(jnp.int32)[:, None]
    places = jnp.arange(cap)[None, :]
    filled = places < counts[:, None]
    source = jnp.where(filled, starts[:, None] + places, -1).astype(jnp.int32)
    taken = jnp.take(row_variant_index, jnp.maximum(source, 0))
    var_send = jnp.where(filled, taken - jnp.arange(pools)[:, None] * variants, -1)
    var_send = jnp.broadcast_to(
        var_send.reshape(slots, 1).astype(BF16), (slots, LANES)
    )
    place = diagonal_block_index[0][:, 0] - lax.axis_index("tensor") * per_shard
    place_tab = jnp.zeros((LANES, LANES), BF16).at[:variants].set(
        jnp.broadcast_to(place.astype(BF16)[:, None], (variants, LANES))
    )

    vmem = pl.BlockSpec(memory_space=pltpu.VMEM)
    hbm = pl.BlockSpec(memory_space=pl.ANY)
    packed = (slots // reps, LANES)
    dma = pltpu.SemaphoreType.DMA
    out = pl.pallas_call(
        functools.partial(fused, (n, pools, sections, rank, cw, tile)),
        out_shape=jax.ShapeDtypeStruct((rows, width), BF16),
        in_specs=[vmem, vmem, hbm, hbm, hbm, vmem, vmem, vmem, vmem, vmem],
        out_specs=vmem,
        scratch_shapes=[
            pltpu.VMEM(((n + 1) * groups, rows, cw), BF16),
            pltpu.VMEM((2, 2, width, cw), BF16),
            pltpu.VMEM((rows, cw), F32),
            pltpu.VMEM((groups, rows, cw), F32),
            pltpu.VMEM((slots, max(width, low_rows)), BF16),
            pltpu.VMEM((slots, width), BF16),
            pltpu.VMEM((slots, width), BF16),
            pltpu.VMEM((low_rows, width), BF16),
            pltpu.VMEM((slots, LANES), BF16),
            pltpu.VMEM((rows, slots), BF16),
            pltpu.VMEM((rows, width), BF16),
            pltpu.VMEM((slots, LANES), F32),
            pltpu.VMEM(packed, F32),
            pltpu.VMEM(packed, BF16),
            pltpu.VMEM(packed, BF16),
            pltpu.VMEM(packed, BF16),
            pltpu.VMEM(packed, BF16),
            pltpu.VMEM((slots, LANES), F32),
            pltpu.VMEM((slots, LANES), F32),
            pltpu.VMEM((slots, LANES), F32),
            dma((2, 2)),
            dma,
            dma(((n + 1) * groups,)),
            dma(((n + 1) * groups,)),
            dma((pools,)),
            dma((pools,)),
            dma((pools,)),
            dma((pools,)),
            dma((groups, pools)),
            dma((groups, pools)),
            dma((2,)),
            dma((2,)),
            dma((groups,)),
            dma((groups,)),
        ],
        compiler_params=pltpu.CompilerParams(
            collective_id=0, has_side_effects=True, vmem_limit_bytes=60 * 1024 * 1024
        ),
        cost_estimate=pl.CostEstimate(
            flops=2 * rows * width * width * n + 4 * slots * low_rows * width,
            bytes_accessed=2 * (width * width * n + 2 * low_rows * width),
            transcendentals=0,
        ),
    )(
        feat, hidden_input, weight, down.reshape(low_rows, width), up.reshape(low_rows, width),
        mats.reshape(variants * block, block), source.reshape(slots, 1), slot, var_send, place_tab,
    )
    return out[None]


def solution(mesh):
    return jax.shard_map(
        functools.partial(per_device, mesh),
        mesh=mesh,
        in_specs=(
            P("pool", "tensor"),
            P("section", "pool", "tensor"),
            P("section", "tensor", None),
            P("section", "pool", None, "tensor"),
            P("section", "pool", None, "tensor"),
            P("section", "pool", "tensor", None, None),
            P("section", "pool", "tensor"),
            P("pool"),
        ),
        out_specs=P("section", "pool", "tensor"),
        check_vma=False,
    )
```

```python
import functools
import math

import jax
import jax.numpy as jnp
from jax import lax
from jax.experimental import pallas as pl
from jax.experimental.pallas import tpu as pltpu
from jax.sharding import PartitionSpec as P

LANES = 128
LAG = 2
WINDOW = 4
BF16 = jnp.bfloat16
F32 = jnp.float32


def remote(src, dst, send_sem, recv_sem, **where):
    return pltpu.make_async_remote_copy(
        src_ref=src,
        dst_ref=dst,
        send_sem=send_sem,
        recv_sem=recv_sem,
        device_id=where,
        device_id_type=pl.DeviceIdType.MESH,
    )


def fused(
    cfg,
    feat, hidden, weight, down, up, mats, row_var, place_of,
    out,
    rbuf, wbuf, tmp, acc, sendf, recvf, retf, lowbuf, varbuf, comb, secbuf,
    lracc, lrp, pre_in, suf_in, pre_out, suf_out, yterm, placef, pickb, var_send,
    w_sem, low_sem, rs_send, rs_recv, a2a_send, a2a_recv, var_ssem, var_rsem,
    ret_send, ret_recv, lr_send, lr_recv, sec_send, sec_recv,
):
    n, pools, sections, rank, cw, tile = cfg
    rows, width = feat.shape
    groups = width // cw
    slots = recvf.shape[0]
    cap = slots // pools
    reps = LANES // rank
    low_rows = lowbuf.shape[0]
    i = lax.axis_index("tensor")
    me = lax.axis_index("pool")
    sec = lax.axis_index("section")
    seqs = (n - 1) * groups
    plus_at = (n - 1 - i) * groups + LAG * i
    minus_at = i * groups + LAG * (n - 1 - i)
    plus_first = (i > 0) & ((i == n - 1) | (plus_at <= minus_at))

    def low_copy(src):
        return pltpu.make_async_copy(src, lowbuf, low_sem)

    def parts(step, direction):
        lag_pos = i if direction == 0 else n - 1 - i
        seq = step - LAG * lag_pos
        valid = (seq >= 0) & (seq < seqs)
        seq = jnp.clip(seq, 0, seqs - 1)
        phase, chunk = seq // groups, seq % groups
        if direction == 0:
            target = n - 1 - phase
            sends = valid & (target > i)
            keeps = valid & (target == i)
            first = keeps & plus_first
            receives = i > 0
            index = target * groups + chunk
        else:
            target = phase
            sends = valid & (target < i)
            keeps = valid & (target == i)
            first = keeps & jnp.logical_not(plus_first)
            receives = i < n - 1
            index = jnp.where(target == i, n, target) * groups + chunk
        return seq, target, chunk, sends, keeps, first, receives, index

    def weight_copy(step, direction):
        _, target, chunk, _, _, _, _, _ = parts(step, direction)
        column = pl.multiple_of(target * width + chunk * cw, cw)
        return pltpu.make_async_copy(
            weight.at[:, pl.ds(column, cw)],
            wbuf.at[step % 2, direction],
            w_sem.at[step % 2, direction],
        )

    def fetch(step):
        for direction in range(2):
            _, _, _, sends, _, first, _, _ = parts(step, direction)

            @pl.when(sends | first)
            def _():
                weight_copy(step, direction).start()

    def rs_copy(direction, index):
        to = i + 1 if direction == 0 else i - 1
        return remote(
            rbuf.at[index], rbuf.at[index], rs_send.at[index], rs_recv.at[index],
            tensor=jnp.clip(to, 0, n - 1),
        )

    def rs_out(direction, seq):
        phase, chunk = seq // groups, seq % groups
        target = n - 1 - phase if direction == 0 else phase
        index = target * groups + chunk
        to = i + 1 if direction == 0 else i - 1
        landing = index
        if direction == 1:
            landing = jnp.where(target == to, n, target) * groups + chunk
        return remote(
            rbuf.at[index], rbuf.at[landing], rs_send.at[index], rs_recv.at[landing],
            tensor=jnp.clip(to, 0, n - 1),
        )

    def step_body(step):
        @pl.when(step + 1 < total_steps)
        def _():
            fetch(step + 1)

        for direction in range(2):
            seq, _, chunk, sends, keeps, first, receives, index = parts(step, direction)

            @pl.when(sends | first)
            def _():
                weight_copy(step, direction).wait()
                tmp[...] = jnp.dot(
                    feat[...], wbuf[step % 2, direction], preferred_element_type=F32
                )

            @pl.when((sends | keeps) & receives)
            def _():
                rs_copy(direction, index).wait_recv()

            @pl.when(sends)
            def _():
                @pl.when(receives)
                def _():
                    rbuf[index] = (tmp[...] + rbuf[index].astype(F32)).astype(BF16)

                @pl.when(jnp.logical_not(receives))
                def _():
                    rbuf[index] = tmp[...].astype(BF16)

                @pl.when(seq >= WINDOW)
                def _():
                    rs_out(direction, seq - WINDOW).wait_send()

                rs_out(direction, seq).start()

            @pl.when(first & receives)
            def _():
                acc[chunk] = tmp[...] + rbuf[index].astype(F32)

            @pl.when(first & jnp.logical_not(receives))
            def _():
                acc[chunk] = tmp[...]

            @pl.when(keeps & receives & jnp.logical_not(first))
            def _():
                acc[chunk] = acc[chunk] + rbuf[index].astype(F32)

    per_step = 2
    tiles = low_rows // tile
    tiles_per_step = 3
    adapt_at = max(3, 5 * seqs // 12)
    hops_at = adapt_at + tiles // tiles_per_step
    served_at = hops_at + max(n - 1, 2)
    finals = [
        max((n - 1 - p) * groups + LAG * p, p * groups + LAG * (n - 1 - p), served_at)
        for p in range(n)
    ]
    total_steps = max(finals) + groups
    final_at = jnp.maximum(jnp.maximum(plus_at, minus_at), served_at)

    def sec_copy(chunk):
        cols = pl.ds(pl.multiple_of(chunk * cw, cw), cw)
        return remote(
            out.at[:, cols], secbuf.at[:, cols], sec_send.at[chunk], sec_recv.at[chunk],
            section=jnp.minimum(sec + 1, sections - 1),
        )

    def ret_copy(chunk, d):
        to = (me + d) % pools
        cols = pl.ds(pl.multiple_of(chunk * cw, cw), cw)
        return remote(
            recvf.at[pl.ds(pl.multiple_of(to * cap, cap), cap), cols],
            retf.at[pl.ds(pl.multiple_of(me * cap, cap), cap), cols],
            ret_send.at[chunk, to],
            ret_recv.at[chunk, me],
            pool=to,
        )

    def ret_arrival(chunk, d):
        owner = (me + d) % pools
        cols = pl.ds(pl.multiple_of(chunk * cw, cw), cw)
        return remote(
            recvf.at[pl.ds(pl.multiple_of(owner * cap, cap), cap), cols],
            retf.at[pl.ds(pl.multiple_of(owner * cap, cap), cap), cols],
            ret_send.at[chunk, owner],
            ret_recv.at[chunk, owner],
            pool=owner,
        )

    def finish(chunk):
        cols = pl.ds(pl.multiple_of(chunk * cw, cw), cw)
        for d in range(1, pools):
            ret_arrival(chunk, d).wait_recv()
        tmp[...] = acc[chunk] + jnp.dot(comb[...], retf[:, cols], preferred_element_type=F32)

        @pl.when(sec == 0)
        def _():
            out[:, cols] = (hidden[:, cols].astype(F32) + tmp[...]).astype(BF16)

        @pl.when(sec > 0)
        def _():
            sec_copy(chunk).wait_recv()
            out[:, cols] = (secbuf[:, cols].astype(F32) + tmp[...]).astype(BF16)

        @pl.when(sec < sections - 1)
        def _():
            sec_copy(chunk).start()

    def steps(first, last):
        @pl.loop(first, last)
        def _(step):
            step_body(step)
            chunk = step - final_at

            @pl.when((chunk >= 0) & (chunk < groups))
            def _():
                finish(chunk)

    def row_copy(d):
        to = (me + d) % pools
        return remote(
            sendf.at[pl.ds(pl.multiple_of(to * cap, cap), cap), pl.ds(0, width)],
            recvf.at[pl.ds(pl.multiple_of(me * cap, cap), cap)],
            a2a_send.at[to], a2a_recv.at[me], pool=to,
        )

    def var_copy(d):
        to = (me + d) % pools
        return remote(
            var_send.at[pl.ds(pl.multiple_of(to * cap, cap), cap)],
            varbuf.at[pl.ds(pl.multiple_of(me * cap, cap), cap)],
            var_ssem.at[to], var_rsem.at[me], pool=to,
        )

    def arrival(d):
        owner = (me + d) % pools
        block = pl.ds(pl.multiple_of(owner * cap, cap), cap)
        return (
            remote(sendf.at[block, pl.ds(0, width)], recvf.at[block], a2a_send.at[owner], a2a_recv.at[owner], pool=owner),
            remote(var_send.at[block], varbuf.at[block], var_ssem.at[owner], var_rsem.at[owner], pool=owner),
        )

    def pre_copy():
        return remote(pre_out, pre_in, lr_send.at[0], lr_recv.at[0],
                      tensor=jnp.minimum(i + 1, n - 1))

    def suf_copy():
        return remote(suf_out, suf_in, lr_send.at[1], lr_recv.at[1],
                      tensor=jnp.maximum(i - 1, 0))

    barrier = pltpu.get_barrier_semaphore()
    for d in range(1, pools):
        pl.semaphore_signal(barrier, inc=1, device_id={"pool": (me + d) % pools},
                            device_id_type=pl.DeviceIdType.MESH)
    for d in range(1, sections):
        pl.semaphore_signal(barrier, inc=1, device_id={"section": (sec + d) % sections},
                            device_id_type=pl.DeviceIdType.MESH)

    @pl.when(i > 0)
    def _():
        pl.semaphore_signal(barrier, inc=1, device_id={"tensor": jnp.maximum(i - 1, 0)},
                            device_id_type=pl.DeviceIdType.MESH)

    @pl.when(i < n - 1)
    def _():
        pl.semaphore_signal(barrier, inc=1, device_id={"tensor": jnp.minimum(i + 1, n - 1)},
                            device_id_type=pl.DeviceIdType.MESH)

    fetch(0)
    low_copy(down).start()
    pl.semaphore_wait(
        barrier,
        pools - 1 + sections - 1 + (i > 0).astype(jnp.int32) + (i < n - 1).astype(jnp.int32),
    )

    steps(0, 2)

    variants = low_rows // rank
    ids = row_var[...]
    place_in_block = lax.broadcasted_iota(jnp.int32, (1, rows), 1)

    def picks_of(owner):
        mine = (ids >= owner * variants) & (ids < (owner + 1) * variants)
        start = jnp.sum((ids < owner * variants).astype(F32), axis=1, keepdims=True)
        position = jnp.where(mine, place_in_block.astype(F32) - start, -1.0)
        slot = lax.broadcasted_iota(jnp.int32, (cap, rows), 0).astype(F32)
        return (slot == position).astype(F32)

    def dispatch(owner, into, vars_into):
        block = pl.ds(pl.multiple_of(owner * cap, cap), cap)
        pick = picks_of(owner).astype(BF16)
        local = (ids - owner * variants + 1).astype(F32).astype(BF16)
        vars_into[block, :] = (
            lax.dot_general(
                pick, jnp.broadcast_to(local, (LANES, rows)),
                (((1,), (1,)), ((), ())), preferred_element_type=F32,
            )
            - 1.0
        ).astype(BF16)

        @pl.loop(0, groups)
        def _(chunk):
            cols = pl.ds(pl.multiple_of(chunk * cw, cw), cw)
            into[block, cols] = jnp.dot(
                pick, feat[:, cols], preferred_element_type=F32
            ).astype(BF16)

    @pl.loop(1, pools)
    def _(d):
        dispatch((me + d) % pools, sendf, var_send)
        row_copy(d).start()
        var_copy(d).start()

    steps(2, 3)
    own = pl.ds(pl.multiple_of(me * cap, cap), cap)
    dispatch(me, recvf, varbuf)
    for q in range(pools):
        comb[:, q * cap:(q + 1) * cap] = picks_of(q).T.astype(BF16)

    steps(3, adapt_at)

    for d in range(1, pools):
        rows_in, vars_in = arrival(d)
        rows_in.wait_recv()
        vars_in.wait_recv()
    low_copy(down).wait()
    lane = lax.broadcasted_iota(jnp.int32, (slots, LANES), 1)
    lane_var = (lane // rank).astype(F32)
    per_tile = tile // LANES
    lracc[...] = jnp.zeros_like(lracc)

    @pl.loop(0, tiles)
    def _(t):
        product = lax.dot_general(
            recvf[...], lowbuf[pl.ds(pl.multiple_of(t * tile, tile), tile), :],
            (((1,), (1,)), ((), ())), preferred_element_type=F32,
        )
        base_var = varbuf[...].astype(F32) - lane_var
        total = lracc[...]
        for b in range(per_tile):
            wanted = ((t * per_tile + b) * reps).astype(F32)
            total = total + jnp.where(
                base_var == wanted, product[:, b * LANES:(b + 1) * LANES], 0.0
            )
        lracc[...] = total

        @pl.when(t % tiles_per_step == tiles_per_step - 1)
        def _():
            at = adapt_at + t // tiles_per_step
            steps(at, at + 1)

    low_copy(up).start()
    folded = lracc[...]
    for j in range(1, reps):
        folded = folded + pltpu.roll(lracc[...], j * rank, 1)
    packed_rows = slots // reps
    lane_p = lax.broadcasted_iota(jnp.int32, (packed_rows, LANES), 1) // rank
    packed = jnp.zeros((packed_rows, LANES), F32)
    for j in range(reps):
        packed = jnp.where(lane_p == j, folded[j * packed_rows:(j + 1) * packed_rows], packed)
    lrp[...] = packed

    def hop(h):
        @pl.when(i == h)
        def _():
            @pl.when(i > 0)
            def _():
                pre_copy().wait_recv()

            @pl.when(i == 0)
            def _():
                pre_out[...] = lrp[...].astype(BF16)

            @pl.when((i > 0) & (i < n - 1))
            def _():
                pre_out[...] = (lrp[...] + pre_in[...].astype(F32)).astype(BF16)

            @pl.when(i < n - 1)
            def _():
                pre_copy().start()

        @pl.when(n - 1 - i == h)
        def _():
            @pl.when(i < n - 1)
            def _():
                suf_copy().wait_recv()

            @pl.when(i == n - 1)
            def _():
                suf_out[...] = lrp[...].astype(BF16)

            @pl.when((i > 0) & (i < n - 1))
            def _():
                suf_out[...] = (lrp[...] + suf_in[...].astype(F32)).astype(BF16)

            @pl.when(i > 0)
            def _():
                suf_copy().start()

    hop(0)

    steps(hops_at, hops_at + 1)
    hop(1)

    lane_v = lax.broadcasted_iota(jnp.int32, (slots, variants), 1).astype(F32)
    hot = (varbuf[:, 0:variants].astype(F32) == lane_v).astype(F32).astype(BF16)
    place = (place_of[...] - i * (width // LANES)).astype(F32).astype(BF16)
    placef[...] = lax.dot_general(
        hot, jnp.broadcast_to(place, (LANES, variants)),
        (((1,), (1,)), ((), ())), preferred_element_type=F32,
    )
    yterm[...] = jnp.zeros_like(yterm)

    @pl.loop(0, width // LANES)
    def _(p):
        block = recvf[:, pl.ds(pl.multiple_of(p * LANES, LANES), LANES)].astype(F32)
        yterm[...] = jnp.where(placef[...] == p.astype(F32), block, yterm[...])

    pickb[...] = yterm[...]
    steps(hops_at + 1, hops_at + 2)
    hop(2)
    yterm[...] = jnp.zeros_like(yterm)
    bunch = math.gcd(4, mats.shape[0] // LANES)
    bunch_rows = bunch * LANES

    @pl.loop(0, mats.shape[0] // bunch_rows)
    def _(g):
        masked = [
            jnp.where(
                varbuf[...].astype(F32) == (g * bunch + b).astype(F32), pickb[...], 0.0
            ).astype(BF16)
            for b in range(bunch)
        ]
        yterm[...] += jnp.dot(
            jnp.concatenate(masked, axis=1),
            mats[pl.ds(pl.multiple_of(g * bunch_rows, bunch_rows), bunch_rows), :],
            preferred_element_type=F32,
        )

    @pl.loop(3, max(n, 3))
    def _(h):
        steps(hops_at + h - 1, hops_at + h)
        hop(h)

    @pl.when(i > 0)
    def _():
        lrp[...] += pre_in[...].astype(F32)

    @pl.when(i < n - 1)
    def _():
        lrp[...] += suf_in[...].astype(F32)

    for d in range(1, pools):
        row_copy(d).wait_send()
        var_copy(d).wait_send()
    for j in range(reps):
        mine = jnp.where(lane_p == j, lrp[...], 0.0)
        spread = mine
        for k in range(1, reps):
            spread = spread + pltpu.roll(mine, k * rank, 1)
        spread = spread.astype(BF16)
        block = pl.ds(j * packed_rows, packed_rows)
        base_var = varbuf[block, :].astype(F32) - lane_p.astype(F32)
        for b in range(low_rows // LANES):
            sendf[block, b * LANES:(b + 1) * LANES] = jnp.where(
                base_var == float(b * reps), spread, 0.0
            ).astype(BF16)
    low_copy(up).wait()

    def serve(chunk):
        cols = pl.ds(pl.multiple_of(chunk * cw, cw), cw)
        answer = jnp.dot(sendf[:, 0:low_rows], lowbuf[:, cols], preferred_element_type=F32)
        placed = [
            jnp.where(placef[...] == (chunk * (cw // LANES) + b).astype(F32), yterm[...], 0.0)
            for b in range(cw // LANES)
        ]
        recvf[:, cols] = (answer + jnp.concatenate(placed, axis=1)).astype(BF16)
        for d in range(1, pools):
            ret_copy(chunk, d).start()
        retf[own, cols] = recvf[own, cols]

    per_step = 2
    @pl.loop(0, groups)
    def _(chunk):
        serve(chunk)

        @pl.when(chunk % per_step == per_step - 1)
        def _():
            at = served_at + chunk // per_step
            steps(at, at + 1)

    steps(served_at + groups // per_step, total_steps)

    for direction in range(2):
        count = ((n - 1 - i) if direction == 0 else i) * groups

        @pl.loop(jnp.maximum(count - WINDOW, 0), count)
        def _(seq):
            rs_out(direction, seq).wait_send()

    @pl.when(i < n - 1)
    def _():
        pre_copy().wait_send()

    @pl.when(i > 0)
    def _():
        suf_copy().wait_send()

    @pl.loop(0, groups)
    def _(chunk):
        for d in range(1, pools):
            ret_copy(chunk, d).wait_send()

        @pl.when(sec < sections - 1)
        def _():
            sec_copy(chunk).wait_send()


def per_device(
    mesh,
    hidden_input,
    attention_output,
    projection_weight,
    lowrank_down_factor,
    lowrank_up_factor,
    residual_block_mats,
    diagonal_block_index,
    row_variant_index,
):
    n, pools, sections = mesh.shape["tensor"], mesh.shape["pool"], mesh.shape["section"]
    feat, weight = attention_output[0], projection_weight[0]
    down, up, mats = lowrank_down_factor[0], lowrank_up_factor[0], residual_block_mats[0][:, 0]
    rows, width = feat.shape
    variants, rank, _ = down.shape
    block = mats.shape[-1]
    low_rows = variants * rank
    cap = rows // 2
    slots = pools * cap
    cw = min(256, width)
    groups = width // cw
    tile = min(256, low_rows)
    reps = LANES // rank

    vmem = pl.BlockSpec(memory_space=pltpu.VMEM)
    hbm = pl.BlockSpec(memory_space=pl.ANY)
    packed = (slots // reps, LANES)
    dma = pltpu.SemaphoreType.DMA
    out = pl.pallas_call(
        functools.partial(fused, (n, pools, sections, rank, cw, tile)),
        out_shape=jax.ShapeDtypeStruct((rows, width), BF16),
        in_specs=[vmem, vmem, hbm, hbm, hbm, vmem, vmem, vmem],
        out_specs=vmem,
        scratch_shapes=[
            pltpu.VMEM(((n + 1) * groups, rows, cw), BF16),
            pltpu.VMEM((2, 2, width, cw), BF16),
            pltpu.VMEM((rows, cw), F32),
            pltpu.VMEM((groups, rows, cw), F32),
            pltpu.VMEM((slots, max(width, low_rows)), BF16),
            pltpu.VMEM((slots, width), BF16),
            pltpu.VMEM((slots, width), BF16),
            pltpu.VMEM((low_rows, width), BF16),
            pltpu.VMEM((slots, LANES), BF16),
            pltpu.VMEM((rows, slots), BF16),
            pltpu.VMEM((rows, width), BF16),
            pltpu.VMEM((slots, LANES), F32),
            pltpu.VMEM(packed, F32),
            pltpu.VMEM(packed, BF16),
            pltpu.VMEM(packed, BF16),
            pltpu.VMEM(packed, BF16),
            pltpu.VMEM(packed, BF16),
            pltpu.VMEM((slots, LANES), F32),
            pltpu.VMEM((slots, LANES), F32),
            pltpu.VMEM((slots, LANES), F32),
            pltpu.VMEM((slots, LANES), BF16),
            dma((2, 2)),
            dma,
            dma(((n + 1) * groups,)),
            dma(((n + 1) * groups,)),
            dma((pools,)),
            dma((pools,)),
            dma((pools,)),
            dma((pools,)),
            dma((groups, pools)),
            dma((groups, pools)),
            dma((2,)),
            dma((2,)),
            dma((groups,)),
            dma((groups,)),
        ],
        compiler_params=pltpu.CompilerParams(
            collective_id=0, has_side_effects=True, vmem_limit_bytes=60 * 1024 * 1024
        ),
        cost_estimate=pl.CostEstimate(
            flops=2 * rows * width * width * n + 4 * slots * low_rows * width,
            bytes_accessed=2 * (width * width * n + 2 * low_rows * width),
            transcendentals=0,
        ),
    )(
        feat, hidden_input, weight, down.reshape(low_rows, width), up.reshape(low_rows, width),
        mats.reshape(variants * block, block), row_variant_index.reshape(1, rows),
        diagonal_block_index[0].reshape(1, variants),
    )
    return out[None]


def solution(mesh):
    return jax.shard_map(
        functools.partial(per_device, mesh),
        mesh=mesh,
        in_specs=(
            P("pool", "tensor"),
            P("section", "pool", "tensor"),
            P("section", "tensor", None),
            P("section", "pool", None, "tensor"),
            P("section", "pool", None, "tensor"),
            P("section", "pool", "tensor", None, None),
            P("section", "pool", "tensor"),
            P("pool"),
        ),
        out_specs=P("section", "pool", "tensor"),
        check_vma=False,
    )
```

```python
import functools
import math

import jax
import jax.numpy as jnp
from jax import lax
from jax.experimental import pallas as pl
from jax.experimental.pallas import tpu as pltpu
from jax.sharding import PartitionSpec as P

LANES = 128
LAG = 2
WINDOW = 4
NEAR_WINDOW = 2
BF16 = jnp.bfloat16
F32 = jnp.float32


def remote(src, dst, send_sem, recv_sem, **where):
    return pltpu.make_async_remote_copy(
        src_ref=src,
        dst_ref=dst,
        send_sem=send_sem,
        recv_sem=recv_sem,
        device_id=where,
        device_id_type=pl.DeviceIdType.MESH,
    )


def fused(
    cfg,
    feat_in, hidden_in, weight, down, up, mats_in, row_var, place_of,
    out_hbm,
    feat, hidden, mats, out,
    rbuf, wbuf, tmp, acc, sendf, recvf, retf, lowbuf, varbuf, comb, secbuf,
    lracc, lrp, pre_in, suf_in, pre_out, suf_out, yterm, placef, pickb, var_send,
    w_sem, low_sem, rs_send, rs_recv, a2a_send, a2a_recv, var_ssem, var_rsem,
    ret_send, ret_recv, lr_send, lr_recv, sec_send, sec_recv, in_sem, out_sem,
):
    n, pools, sections, rank, cw, tile = cfg
    rows, width = feat.shape
    groups = width // cw
    slots = recvf.shape[0]
    cap = slots // pools
    reps = LANES // rank
    low_rows = lowbuf.shape[0]
    i = lax.axis_index("tensor")
    me = lax.axis_index("pool")
    sec = lax.axis_index("section")
    seqs = (n - 1) * groups
    plus_at = (n - 1 - i) * groups + LAG * i
    minus_at = i * groups + LAG * (n - 1 - i)
    plus_first = (i > 0) & ((i == n - 1) | (plus_at <= minus_at))

    def low_copy(src):
        return pltpu.make_async_copy(src, lowbuf, low_sem)

    def parts(step, direction):
        lag_pos = i if direction == 0 else n - 1 - i
        seq = step - LAG * lag_pos
        valid = (seq >= 0) & (seq < seqs)
        seq = jnp.clip(seq, 0, seqs - 1)
        phase, chunk = seq // groups, seq % groups
        if direction == 0:
            target = n - 1 - phase
            sends = valid & (target > i)
            keeps = valid & (target == i)
            first = keeps & plus_first
            receives = i > 0
            index = target * groups + chunk
        else:
            target = phase
            sends = valid & (target < i)
            keeps = valid & (target == i)
            first = keeps & jnp.logical_not(plus_first)
            receives = i < n - 1
            index = jnp.where(target == i, n, target) * groups + chunk
        return seq, target, chunk, sends, keeps, first, receives, index

    def weight_copy(step, direction):
        _, target, chunk, _, _, _, _, _ = parts(step, direction)
        column = pl.multiple_of(target * width + chunk * cw, cw)
        return pltpu.make_async_copy(
            weight.at[:, pl.ds(column, cw)],
            wbuf.at[step % 2, direction],
            w_sem.at[step % 2, direction],
        )

    def fetch(step):
        for direction in range(2):
            _, _, _, sends, _, first, _, _ = parts(step, direction)

            @pl.when(sends | first)
            def _():
                weight_copy(step, direction).start()

    def rs_copy(direction, index):
        to = i + 1 if direction == 0 else i - 1
        return remote(
            rbuf.at[index], rbuf.at[index], rs_send.at[index], rs_recv.at[index],
            tensor=jnp.clip(to, 0, n - 1),
        )

    def rs_out(direction, seq):
        phase, chunk = seq // groups, seq % groups
        target = n - 1 - phase if direction == 0 else phase
        index = target * groups + chunk
        to = i + 1 if direction == 0 else i - 1
        landing = index
        if direction == 1:
            landing = jnp.where(target == to, n, target) * groups + chunk
        return remote(
            rbuf.at[index], rbuf.at[landing], rs_send.at[index], rs_recv.at[landing],
            tensor=jnp.clip(to, 0, n - 1),
        )

    def left_by(seq):
        near = jnp.where(seq >= adapt_at, jnp.minimum(seq, served_at) - NEAR_WINDOW, 0)
        return jnp.maximum(jnp.maximum(seq - WINDOW, near), 0)

    def step_body(step):
        @pl.when(step + 1 < total_steps)
        def _():
            fetch(step + 1)

        for direction in range(2):
            seq, _, chunk, sends, keeps, first, receives, index = parts(step, direction)

            @pl.when(sends | first)
            def _():
                weight_copy(step, direction).wait()
                tmp[...] = jnp.dot(
                    feat[...], wbuf[step % 2, direction], preferred_element_type=F32
                )

            @pl.when((sends | keeps) & receives)
            def _():
                rs_copy(direction, index).wait_recv()

            @pl.when(sends)
            def _():
                @pl.when(receives)
                def _():
                    rbuf[index] = (tmp[...] + rbuf[index].astype(F32)).astype(BF16)

                @pl.when(jnp.logical_not(receives))
                def _():
                    rbuf[index] = tmp[...].astype(BF16)

                @pl.loop(left_by(seq - 1), left_by(seq))
                def _(earlier):
                    rs_out(direction, earlier).wait_send()

                rs_out(direction, seq).start()

            @pl.when(first & receives)
            def _():
                acc[chunk] = tmp[...] + rbuf[index].astype(F32)

            @pl.when(first & jnp.logical_not(receives))
            def _():
                acc[chunk] = tmp[...]

            @pl.when(keeps & receives & jnp.logical_not(first))
            def _():
                acc[chunk] = acc[chunk] + rbuf[index].astype(F32)

    per_step = 2
    tiles = low_rows // tile
    tiles_per_step = 3
    adapt_at = max(3, 3 * seqs // 8)
    hops_at = adapt_at + tiles // tiles_per_step
    served_at = hops_at + max(n - 2, 1)
    finals = [
        max((n - 1 - p) * groups + LAG * p, p * groups + LAG * (n - 1 - p), served_at)
        for p in range(n)
    ]
    total_steps = max(finals) + groups
    final_at = jnp.maximum(jnp.maximum(plus_at, minus_at), served_at)

    def sec_copy(chunk):
        cols = pl.ds(pl.multiple_of(chunk * cw, cw), cw)
        return remote(
            out.at[:, cols], secbuf.at[:, cols], sec_send.at[chunk], sec_recv.at[chunk],
            section=jnp.minimum(sec + 1, sections - 1),
        )

    def ret_copy(chunk, d):
        to = (me + d) % pools
        cols = pl.ds(pl.multiple_of(chunk * cw, cw), cw)
        return remote(
            recvf.at[pl.ds(pl.multiple_of(to * cap, cap), cap), cols],
            retf.at[pl.ds(pl.multiple_of(me * cap, cap), cap), cols],
            ret_send.at[chunk, to],
            ret_recv.at[chunk, me],
            pool=to,
        )

    def ret_arrival(chunk, d):
        owner = (me + d) % pools
        cols = pl.ds(pl.multiple_of(chunk * cw, cw), cw)
        return remote(
            recvf.at[pl.ds(pl.multiple_of(owner * cap, cap), cap), cols],
            retf.at[pl.ds(pl.multiple_of(owner * cap, cap), cap), cols],
            ret_send.at[chunk, owner],
            ret_recv.at[chunk, owner],
            pool=owner,
        )

    def out_copy(chunk):
        cols = pl.ds(pl.multiple_of(chunk * cw, cw), cw)
        return pltpu.make_async_copy(out.at[:, cols], out_hbm.at[:, cols], out_sem.at[chunk])

    def finish(chunk):
        cols = pl.ds(pl.multiple_of(chunk * cw, cw), cw)
        for d in range(1, pools):
            ret_arrival(chunk, d).wait_recv()
        tmp[...] = acc[chunk] + jnp.dot(comb[...], retf[:, cols], preferred_element_type=F32)

        @pl.when(sec == 0)
        def _():
            out[:, cols] = (hidden[:, cols].astype(F32) + tmp[...]).astype(BF16)

        @pl.when(sec > 0)
        def _():
            sec_copy(chunk).wait_recv()
            out[:, cols] = (secbuf[:, cols].astype(F32) + tmp[...]).astype(BF16)

        @pl.when(sec < sections - 1)
        def _():
            sec_copy(chunk).start()

        out_copy(chunk).start()

    def steps(first, last):
        @pl.loop(first, last)
        def _(step):
            step_body(step)
            chunk = step - final_at

            @pl.when((chunk >= 0) & (chunk < groups))
            def _():
                finish(chunk)

    def row_copy(d):
        to = (me + d) % pools
        return remote(
            sendf.at[pl.ds(pl.multiple_of(to * cap, cap), cap), pl.ds(0, width)],
            recvf.at[pl.ds(pl.multiple_of(me * cap, cap), cap)],
            a2a_send.at[to], a2a_recv.at[me], pool=to,
        )

    def var_copy(d):
        to = (me + d) % pools
        return remote(
            var_send.at[pl.ds(pl.multiple_of(to * cap, cap), cap)],
            varbuf.at[pl.ds(pl.multiple_of(me * cap, cap), cap)],
            var_ssem.at[to], var_rsem.at[me], pool=to,
        )

    def arrival(d):
        owner = (me + d) % pools
        block = pl.ds(pl.multiple_of(owner * cap, cap), cap)
        return (
            remote(sendf.at[block, pl.ds(0, width)], recvf.at[block], a2a_send.at[owner], a2a_recv.at[owner], pool=owner),
            remote(var_send.at[block], varbuf.at[block], var_ssem.at[owner], var_rsem.at[owner], pool=owner),
        )

    def pre_copy():
        return remote(pre_out, pre_in, lr_send.at[0], lr_recv.at[0],
                      tensor=jnp.minimum(i + 1, n - 1))

    def suf_copy():
        return remote(suf_out, suf_in, lr_send.at[1], lr_recv.at[1],
                      tensor=jnp.maximum(i - 1, 0))

    barrier = pltpu.get_barrier_semaphore()
    for d in range(1, pools):
        pl.semaphore_signal(barrier, inc=1, device_id={"pool": (me + d) % pools},
                            device_id_type=pl.DeviceIdType.MESH)
    for d in range(1, sections):
        pl.semaphore_signal(barrier, inc=1, device_id={"section": (sec + d) % sections},
                            device_id_type=pl.DeviceIdType.MESH)

    @pl.when(i > 0)
    def _():
        pl.semaphore_signal(barrier, inc=1, device_id={"tensor": jnp.maximum(i - 1, 0)},
                            device_id_type=pl.DeviceIdType.MESH)

    @pl.when(i < n - 1)
    def _():
        pl.semaphore_signal(barrier, inc=1, device_id={"tensor": jnp.minimum(i + 1, n - 1)},
                            device_id_type=pl.DeviceIdType.MESH)

    feat_load = pltpu.make_async_copy(feat_in, feat, in_sem.at[0])
    hidden_load = pltpu.make_async_copy(hidden_in, hidden, in_sem.at[1])
    mats_load = pltpu.make_async_copy(mats_in, mats, in_sem.at[2])
    feat_load.start()
    fetch(0)
    mats_load.start()
    hidden_load.start()
    low_copy(down).start()
    pl.semaphore_wait(
        barrier,
        pools - 1 + sections - 1 + (i > 0).astype(jnp.int32) + (i < n - 1).astype(jnp.int32),
    )

    feat_load.wait()
    mats_load.wait()
    hidden_load.wait()
    steps(0, 2)

    variants = low_rows // rank
    ids = row_var[...]
    place_in_block = lax.broadcasted_iota(jnp.int32, (1, rows), 1)

    def picks_of(owner):
        mine = (ids >= owner * variants) & (ids < (owner + 1) * variants)
        start = jnp.sum((ids < owner * variants).astype(F32), axis=1, keepdims=True)
        position = jnp.where(mine, place_in_block.astype(F32) - start, -1.0)
        slot = lax.broadcasted_iota(jnp.int32, (cap, rows), 0).astype(F32)
        return (slot == position).astype(F32)

    def dispatch(owner, into, vars_into):
        block = pl.ds(pl.multiple_of(owner * cap, cap), cap)
        pick = picks_of(owner).astype(BF16)
        local = (ids - owner * variants + 1).astype(F32).astype(BF16)
        vars_into[block, :] = (
            lax.dot_general(
                pick, jnp.broadcast_to(local, (LANES, rows)),
                (((1,), (1,)), ((), ())), preferred_element_type=F32,
            )
            - 1.0
        ).astype(BF16)

        @pl.loop(0, groups)
        def _(chunk):
            cols = pl.ds(pl.multiple_of(chunk * cw, cw), cw)
            into[block, cols] = jnp.dot(
                pick, feat[:, cols], preferred_element_type=F32
            ).astype(BF16)

    @pl.loop(1, pools)
    def _(d):
        dispatch((me + d) % pools, sendf, var_send)
        row_copy(d).start()
        var_copy(d).start()

    steps(2, 3)
    own = pl.ds(pl.multiple_of(me * cap, cap), cap)
    dispatch(me, recvf, varbuf)
    for q in range(pools):
        comb[:, q * cap:(q + 1) * cap] = picks_of(q).T.astype(BF16)

    steps(3, adapt_at)

    for d in range(1, pools):
        rows_in, vars_in = arrival(d)
        rows_in.wait_recv()
        vars_in.wait_recv()
    low_copy(down).wait()
    lane = lax.broadcasted_iota(jnp.int32, (slots, LANES), 1)
    lane_var = (lane // rank).astype(F32)
    per_tile = tile // LANES
    lracc[...] = jnp.zeros_like(lracc)

    @pl.loop(0, tiles)
    def _(t):
        product = lax.dot_general(
            recvf[...], lowbuf[pl.ds(pl.multiple_of(t * tile, tile), tile), :],
            (((1,), (1,)), ((), ())), preferred_element_type=F32,
        )
        base_var = varbuf[...].astype(F32) - lane_var
        total = lracc[...]
        for b in range(per_tile):
            wanted = ((t * per_tile + b) * reps).astype(F32)
            total = total + jnp.where(
                base_var == wanted, product[:, b * LANES:(b + 1) * LANES], 0.0
            )
        lracc[...] = total

        @pl.when(t % tiles_per_step == tiles_per_step - 1)
        def _():
            at = adapt_at + t // tiles_per_step
            steps(at, at + 1)

    low_copy(up).start()
    folded = lracc[...]
    for j in range(1, reps):
        folded = folded + pltpu.roll(lracc[...], j * rank, 1)
    packed_rows = slots // reps
    lane_p = lax.broadcasted_iota(jnp.int32, (packed_rows, LANES), 1) // rank
    packed = jnp.zeros((packed_rows, LANES), F32)
    for j in range(reps):
        packed = jnp.where(lane_p == j, folded[j * packed_rows:(j + 1) * packed_rows], packed)
    lrp[...] = packed

    def hop(h):
        @pl.when(i == h)
        def _():
            @pl.when(i > 0)
            def _():
                pre_copy().wait_recv()

            @pl.when(i == 0)
            def _():
                pre_out[...] = lrp[...].astype(BF16)

            @pl.when((i > 0) & (i < n - 1))
            def _():
                pre_out[...] = (lrp[...] + pre_in[...].astype(F32)).astype(BF16)

            @pl.when(i < n - 1)
            def _():
                pre_copy().start()

        @pl.when(n - 1 - i == h)
        def _():
            @pl.when(i < n - 1)
            def _():
                suf_copy().wait_recv()

            @pl.when(i == n - 1)
            def _():
                suf_out[...] = lrp[...].astype(BF16)

            @pl.when((i > 0) & (i < n - 1))
            def _():
                suf_out[...] = (lrp[...] + suf_in[...].astype(F32)).astype(BF16)

            @pl.when(i > 0)
            def _():
                suf_copy().start()

    hop(0)

    lane_v = lax.broadcasted_iota(jnp.int32, (slots, variants), 1).astype(F32)
    hot = (varbuf[:, 0:variants].astype(F32) == lane_v).astype(F32).astype(BF16)
    place = (place_of[...] - i * (width // LANES)).astype(F32).astype(BF16)
    placef[...] = lax.dot_general(
        hot, jnp.broadcast_to(place, (LANES, variants)),
        (((1,), (1,)), ((), ())), preferred_element_type=F32,
    )
    yterm[...] = jnp.zeros_like(yterm)

    @pl.loop(0, width // LANES)
    def _(p):
        block = recvf[:, pl.ds(pl.multiple_of(p * LANES, LANES), LANES)].astype(F32)
        yterm[...] = jnp.where(placef[...] == p.astype(F32), block, yterm[...])

    pickb[...] = yterm[...]
    hop(1)
    steps(hops_at, hops_at + 1)
    yterm[...] = jnp.zeros_like(yterm)
    bunch = math.gcd(4, mats.shape[0] // LANES)
    bunch_rows = bunch * LANES

    @pl.loop(0, mats.shape[0] // bunch_rows)
    def _(g):
        masked = [
            jnp.where(
                varbuf[...].astype(F32) == (g * bunch + b).astype(F32), pickb[...], 0.0
            ).astype(BF16)
            for b in range(bunch)
        ]
        yterm[...] += jnp.dot(
            jnp.concatenate(masked, axis=1),
            mats[pl.ds(pl.multiple_of(g * bunch_rows, bunch_rows), bunch_rows), :],
            preferred_element_type=F32,
        )

    hop(2)

    @pl.loop(3, max(n, 3))
    def _(h):
        steps(hops_at + h - 2, hops_at + h - 1)
        hop(h)

    @pl.when(i > 0)
    def _():
        lrp[...] += pre_in[...].astype(F32)

    @pl.when(i < n - 1)
    def _():
        lrp[...] += suf_in[...].astype(F32)

    for d in range(1, pools):
        row_copy(d).wait_send()
        var_copy(d).wait_send()
    for j in range(reps):
        mine = jnp.where(lane_p == j, lrp[...], 0.0)
        spread = mine
        for k in range(1, reps):
            spread = spread + pltpu.roll(mine, k * rank, 1)
        spread = spread.astype(BF16)
        block = pl.ds(j * packed_rows, packed_rows)
        base_var = varbuf[block, :].astype(F32) - lane_p.astype(F32)
        for b in range(low_rows // LANES):
            sendf[block, b * LANES:(b + 1) * LANES] = jnp.where(
                base_var == float(b * reps), spread, 0.0
            ).astype(BF16)
    low_copy(up).wait()

    def serve(chunk):
        cols = pl.ds(pl.multiple_of(chunk * cw, cw), cw)
        answer = jnp.dot(sendf[:, 0:low_rows], lowbuf[:, cols], preferred_element_type=F32)
        placed = [
            jnp.where(placef[...] == (chunk * (cw // LANES) + b).astype(F32), yterm[...], 0.0)
            for b in range(cw // LANES)
        ]
        recvf[:, cols] = (answer + jnp.concatenate(placed, axis=1)).astype(BF16)
        for d in range(1, pools):
            ret_copy(chunk, d).start()
        retf[own, cols] = recvf[own, cols]

    per_step = 2
    @pl.loop(0, groups)
    def _(chunk):
        serve(chunk)

        @pl.when(chunk % per_step == per_step - 1)
        def _():
            at = served_at + chunk // per_step
            steps(at, at + 1)

    steps(served_at + groups // per_step, total_steps)

    for direction in range(2):
        count = ((n - 1 - i) if direction == 0 else i) * groups

        @pl.loop(left_by(count - 1), count)
        def _(seq):
            rs_out(direction, seq).wait_send()

    @pl.when(i < n - 1)
    def _():
        pre_copy().wait_send()

    @pl.when(i > 0)
    def _():
        suf_copy().wait_send()

    @pl.loop(0, groups)
    def _(chunk):
        for d in range(1, pools):
            ret_copy(chunk, d).wait_send()

        @pl.when(sec < sections - 1)
        def _():
            sec_copy(chunk).wait_send()

        out_copy(chunk).wait()


def per_device(
    mesh,
    hidden_input,
    attention_output,
    projection_weight,
    lowrank_down_factor,
    lowrank_up_factor,
    residual_block_mats,
    diagonal_block_index,
    row_variant_index,
):
    n, pools, sections = mesh.shape["tensor"], mesh.shape["pool"], mesh.shape["section"]
    feat, weight = attention_output[0], projection_weight[0]
    down, up, mats = lowrank_down_factor[0], lowrank_up_factor[0], residual_block_mats[0][:, 0]
    rows, width = feat.shape
    variants, rank, _ = down.shape
    block = mats.shape[-1]
    low_rows = variants * rank
    cap = rows // 2
    slots = pools * cap
    cw = min(256, width)
    groups = width // cw
    tile = min(256, low_rows)
    reps = LANES // rank

    vmem = pl.BlockSpec(memory_space=pltpu.VMEM)
    hbm = pl.BlockSpec(memory_space=pl.ANY)
    packed = (slots // reps, LANES)
    dma = pltpu.SemaphoreType.DMA
    out = pl.pallas_call(
        functools.partial(fused, (n, pools, sections, rank, cw, tile)),
        out_shape=jax.ShapeDtypeStruct((rows, width), BF16),
        in_specs=[hbm, hbm, hbm, hbm, hbm, hbm, vmem, vmem],
        out_specs=hbm,
        scratch_shapes=[
            pltpu.VMEM((rows, width), BF16),
            pltpu.VMEM((rows, width), BF16),
            pltpu.VMEM((variants * block, block), BF16),
            pltpu.VMEM((rows, width), BF16),
            pltpu.VMEM(((n + 1) * groups, rows, cw), BF16),
            pltpu.VMEM((2, 2, width, cw), BF16),
            pltpu.VMEM((rows, cw), F32),
            pltpu.VMEM((groups, rows, cw), F32),
            pltpu.VMEM((slots, max(width, low_rows)), BF16),
            pltpu.VMEM((slots, width), BF16),
            pltpu.VMEM((slots, width), BF16),
            pltpu.VMEM((low_rows, width), BF16),
            pltpu.VMEM((slots, LANES), BF16),
            pltpu.VMEM((rows, slots), BF16),
            pltpu.VMEM((rows, width), BF16),
            pltpu.VMEM((slots, LANES), F32),
            pltpu.VMEM(packed, F32),
            pltpu.VMEM(packed, BF16),
            pltpu.VMEM(packed, BF16),
            pltpu.VMEM(packed, BF16),
            pltpu.VMEM(packed, BF16),
            pltpu.VMEM((slots, LANES), F32),
            pltpu.VMEM((slots, LANES), F32),
            pltpu.VMEM((slots, LANES), F32),
            pltpu.VMEM((slots, LANES), BF16),
            dma((2, 2)),
            dma,
            dma(((n + 1) * groups,)),
            dma(((n + 1) * groups,)),
            dma((pools,)),
            dma((pools,)),
            dma((pools,)),
            dma((pools,)),
            dma((groups, pools)),
            dma((groups, pools)),
            dma((2,)),
            dma((2,)),
            dma((groups,)),
            dma((groups,)),
            dma((3,)),
            dma((groups,)),
        ],
        compiler_params=pltpu.CompilerParams(
            collective_id=0, has_side_effects=True, vmem_limit_bytes=60 * 1024 * 1024
        ),
        cost_estimate=pl.CostEstimate(
            flops=2 * rows * width * width * n + 4 * slots * low_rows * width,
            bytes_accessed=2 * (width * width * n + 2 * low_rows * width),
            transcendentals=0,
        ),
    )(
        feat, hidden_input, weight, down.reshape(low_rows, width), up.reshape(low_rows, width),
        mats.reshape(variants * block, block), row_variant_index.reshape(1, rows),
        diagonal_block_index[0].reshape(1, variants),
    )
    return out[None]


def solution(mesh):
    return jax.shard_map(
        functools.partial(per_device, mesh),
        mesh=mesh,
        in_specs=(
            P("pool", "tensor"),
            P("section", "pool", "tensor"),
            P("section", "tensor", None),
            P("section", "pool", None, "tensor"),
            P("section", "pool", None, "tensor"),
            P("section", "pool", "tensor", None, None),
            P("section", "pool", "tensor"),
            P("pool"),
        ),
        out_specs=P("section", "pool", "tensor"),
        check_vma=False,
    )
```
